32 devices in a mesh: tm: 4 (over y, core), src: 8 (over z, x).
Axes of the slice: x: 2, y: 2, z: 4, core: 2. Of those that a mesh axis runs over, the one named last changes fastest.
Arguments:
- observed: float32 [131072], P(('tm', 'src')), may hold values from -6 to 6
- att_coef: float32 [4, 4096], P(None, 'tm'), may hold values from -6 to 6
- att_partial: float32 [4, 131072], P(None, ('tm', 'src')), may hold values from -6 to 6
- spline_w: float32 [4, 131072], P(None, ('tm', 'src')), may hold values from 0.05 to 1
- knot_idx: int32 [131072], P(('tm', 'src')), may hold values from 0 to 1023
- src_partial: float32 [5, 131072], P(None, ('tm', 'src')), may hold values from -6 to 6
- src_ids: int32 [131072], P(('tm', 'src')), may hold values from 0 to 16383, as said below
- src_params: float32 [5, 16384], P(None, ('tm', 'src')), may hold values from -6 to 6
- owner_counts: int32 [1024], P(('tm', 'src')), may hold values from 1 to 128, as said below
- cal_partial: float32 [131072, 256], P(('tm', 'src')), may hold values from -6 to 6
- unit_slot: int32 [131072], P(('tm', 'src')), may hold values from 0 to 63
- unit_list: int32 [2048], P(('tm', 'src')), may hold values from 0 to 1023, as said below
Outputs:
- gram: float32 [25, 16384], P(None, ('tm', 'src'))
- src_rhs: float32 [5, 16384], P(None, ('tm', 'src'))
- cal_tiles: float32 [1024, 2, 256], P(('tm', 'src'))
The draws below stay inside these ranges and needn't reach their ends.
Inputs may be any that keep to these rules, and one draw needn't show every extreme that they name: src_ids of slot group o lie in [o * 512, (o + 1) * 512). `owner_counts`: every device has 128 live slots for some owner. `unit_list`: each device names each unit at most once and exactly 2 units of every owner (owner of unit g is g // 32).
All inputs are finite; a program needn't handle non-finite values.
Results may differ from the reference program's by a relative error of at most 0.0003.
Values sent between devices are 32-bit elements; how exact they have to be, the bound alone decides.
A program may use at most 128 MiB of HBM per device.

```python
import jax
import jax.numpy as jnp
from jax import lax

QUAT = 4
ORDER = 4
ASTRO = 5
CALW = 256
CAP = 128
KW = 1024
NS_DEV = 512
UO = 32
CAPU = 2
KOWN = 32
U_DEV = 64
TR_DEV = 4096
NTR = 131072
NK = 4096
NSRC = 16384
NCAL = 1024
N_SRC = 8
DEVICES = 32


def draw_owner_counts(key, part):
    first = jax.random.fold_in(key, 11)
    second = jax.random.fold_in(key, 12)
    counts = jax.random.randint(first, (DEVICES, DEVICES), 1, CAP + 1)
    full_at = jax.random.randint(second, (DEVICES, 1), 0, DEVICES)
    column = jnp.arange(DEVICES, dtype=jnp.int32)[None, :]
    return jnp.where(column == full_at, CAP, counts).reshape(DEVICES * DEVICES).astype(jnp.int32)


def draw_src_ids(key, part):
    trans = jnp.arange(NTR, dtype=jnp.int32)
    owner = trans % TR_DEV // CAP
    local = jax.random.randint(jax.random.fold_in(key, 21), (NTR,), 0, NS_DEV)
    return (owner * NS_DEV + local).astype(jnp.int32)


def draw_unit_list(key, part):
    entry = jnp.arange(U_DEV, dtype=jnp.int32)[None, :]
    group = entry // CAPU
    within = entry % CAPU
    base = jax.random.randint(jax.random.fold_in(key, 31), (DEVICES, 1), 0, DEVICES)
    stride = max(DEVICES // KOWN, 1)
    owner = (base + group * stride) % DEVICES
    offsets = jax.random.randint(jax.random.fold_in(key, 32), (DEVICES, KOWN), 0, UO)
    start = jnp.take_along_axis(offsets, jnp.broadcast_to(group, (DEVICES, U_DEV)), axis=1)
    local = (start + within) % UO
    return (owner * UO + local).reshape(DEVICES * U_DEV).astype(jnp.int32)


def plant(values, own_key, smallest, high):
    longest = values.shape.index(max(values.shape))
    spots = []
    for shift in (0, 1):
        where = [jax.random.randint(jax.random.fold_in(own_key, axis), (), 0, length) for axis, length in enumerate(values.shape)]
        where[longest] = (where[longest] + shift) % values.shape[longest]
        spots.append(tuple(where))
    return values.at[spots[0]].set(smallest).at[spots[1]].set(high)


def steps_of(stream_key, shape, shards, smallest, top_value):
    factor_of = 1.0
    for axis_at, blocks in shards:
        heights = jax.random.uniform(jax.random.fold_in(jax.random.fold_in(stream_key, 6), axis_at), (blocks,), jnp.float32, smallest / len(shards), top_value / len(shards))
        factor_of = factor_of * jnp.repeat(jnp.exp(heights), shape[axis_at] // blocks).reshape((-1,) + (1,) * (len(shape) - 1 - axis_at))
    return factor_of


def normal_values(rng, shape, deviation, limit, shards=(), kind=jnp.bfloat16):
    entries = deviation * jax.random.normal(rng, shape, jnp.float32)
    if shards:
        entries = entries * steps_of(rng, shape, shards, -0.22, 0.18)
    return jnp.clip(entries, -limit, limit).astype(kind)


def setup_inputs(seed: int = 0) -> dict:
    key_of = jax.random.split(jax.random.key(seed), 13)
    observed = normal_values(key_of[0], (NTR,), 1.0, 6.0, ((0, 32),), jnp.float32)
    att_coef = normal_values(key_of[1], (QUAT, NK), 1.0, 6.0, ((1, 4),), jnp.float32)
    att_partial = normal_values(key_of[2], (QUAT, NTR), 0.5, 6.0, ((1, 32),), jnp.float32)
    spline_w = jnp.clip(0.05 + 0.95 * jax.random.uniform(key_of[3], (ORDER, NTR), jnp.float32) ** steps_of(key_of[3], (ORDER, NTR), ((1, 32),), -0.2, 0.2), 0.05, 1.0)
    knot_idx = plant(jax.random.randint(key_of[4], (NTR,), 0, KW), jax.random.fold_in(key_of[4], 1), 0, KW - 1).astype(jnp.int32)
    src_partial = normal_values(key_of[5], (ASTRO, NTR), 1.0, 6.0, ((1, 32),), jnp.float32)
    src_ids = draw_src_ids(jax.random.fold_in(key_of[12], 71), 0)
    src_params = normal_values(key_of[7], (ASTRO, NSRC), 0.5, 6.0, ((1, 32),), jnp.float32)
    owner_counts = draw_owner_counts(jax.random.fold_in(key_of[12], 71), 0)
    cal_partial = normal_values(key_of[9], (NTR, CALW), 1.0, 6.0, ((0, 32),), jnp.float32)
    unit_slot = plant(jax.random.randint(key_of[10], (NTR,), 0, U_DEV), jax.random.fold_in(key_of[10], 1), 0, U_DEV - 1).astype(jnp.int32)
    unit_list = draw_unit_list(jax.random.fold_in(key_of[12], 71), 0)
    return {"observed": observed, "att_coef": att_coef, "att_partial": att_partial, "spline_w": spline_w, "knot_idx": knot_idx, "src_partial": src_partial, "src_ids": src_ids, "src_params": src_params, "owner_counts": owner_counts, "cal_partial": cal_partial, "unit_slot": unit_slot, "unit_list": unit_list}


def reference(observed, att_coef, att_partial, spline_w, knot_idx, src_partial, src_ids, src_params, owner_counts, cal_partial, unit_slot, unit_list):
    trans = jnp.arange(NTR, dtype=jnp.int32)
    device = trans // TR_DEV
    window = device // N_SRC
    padded = jnp.concatenate([att_coef, jnp.zeros((QUAT, ORDER - 1), jnp.float32)], 1)
    att = jnp.zeros((NTR,), jnp.float32)
    for j in range(ORDER):
        columns = jnp.take(padded, (window * KW + knot_idx + j).astype(jnp.int32), axis=1)
        att = att + spline_w[j] * jnp.sum(att_partial * columns, 0)
    owner = (trans % TR_DEV) // CAP
    slot = trans % CAP
    mask = (slot < jnp.take(owner_counts, (device * DEVICES + owner).astype(jnp.int32))).astype(jnp.float32)
    res1 = mask * (observed - att)
    apart = src_partial * mask[None, :]
    picked = jnp.take(src_params, src_ids, axis=1)
    res2 = res1 - jnp.sum(apart * picked, 0)
    prods = jnp.concatenate([(apart[:, None, :] * apart[None, :, :]).reshape(ASTRO * ASTRO, NTR), apart * res2[None, :]], 0)
    summed = jax.ops.segment_sum(prods.T, src_ids, num_segments=NSRC).T
    gram = summed[:ASTRO * ASTRO]
    src_rhs = summed[ASTRO * ASTRO:]

    def per_device(carry, items):
        part, resid, msk, slots, units = items
        onehot = (slots[None, :] == jnp.arange(U_DEV, dtype=jnp.int32)[:, None]).astype(jnp.float32) * msk[None, :]
        rhs = jnp.dot(onehot * resid[None, :], part, precision=lax.Precision.HIGHEST)
        diag = jnp.dot(onehot, part * part, precision=lax.Precision.HIGHEST)
        return carry.at[units].add(jnp.concatenate([rhs, diag], 1)), None

    start = jnp.zeros((NCAL, 2 * CALW), jnp.float32)
    tiles, unused = lax.scan(per_device, start, (cal_partial.reshape(DEVICES, TR_DEV, CALW), res1.reshape(DEVICES, TR_DEV), mask.reshape(DEVICES, TR_DEV), unit_slot.reshape(DEVICES, TR_DEV), unit_list.reshape(DEVICES, U_DEV)))
    return gram, src_rhs, tiles.reshape(NCAL, 2, CALW)
```

```python
import functools

import jax
import jax.numpy as jnp
from jax import lax
from jax.experimental import pallas as pl
from jax.experimental.pallas import tpu as pltpu
from jax.sharding import PartitionSpec as P

ORDER = 4
QUAT = 4
ASTRO = 5
CAP = 128
UO = 32
LANES = 128
GROUP = 4
F32 = jnp.float32
BF16 = jnp.bfloat16
MESH = pl.DeviceIdType.MESH


def halves(x):
    high = x.astype(BF16)
    return high, (x - high.astype(F32)).astype(BF16)


def matmul(a, b):
    return jnp.dot(a, b, preferred_element_type=F32)


def iota(shape, dim):
    return lax.broadcasted_iota(jnp.int32, shape, dim)


def kernel(
    n_time,
    n_src,
    cnt_ref,
    obs_ref,
    coef_ref,
    ap_ref,
    w_ref,
    knot_ref,
    sp_ref,
    ids_ref,
    params_ref,
    uslot_ref,
    ulist_ref,
    cal_hbm,
    gram_ref,
    rhs_ref,
    tiles_ref,
    cal_ref,
    rim_ref,
    amat_ref,
    pmat_ref,
    res_ref,
    live_ref,
    acc_rhs,
    acc_diag,
    acc_src,
    send_a,
    recv_a,
    send_b,
    recv_b,
    cal_sem,
    rim_sems,
    a_sems,
    b_sems,
):
    n = n_time * n_src
    tm = lax.axis_index("tm")
    sc = lax.axis_index("src")
    me = tm * n_src + sc
    transits = obs_ref.shape[1]
    sources = params_ref.shape[1]
    knots = coef_ref.shape[1]
    units = ulist_ref.shape[1]
    width = cal_hbm.shape[1]
    named = units // n
    step = GROUP * CAP
    chunks = transits // step

    def peer(s):
        other = lax.rem(me + s, n)
        return other, (lax.div(other, n_src), lax.rem(other, n_src))

    barrier = pltpu.get_barrier_semaphore()

    @pl.loop(1, n)
    def _(s):
        pl.semaphore_signal(barrier, inc=1, device_id=peer(s)[1], device_id_type=MESH)

    def cal_copy(i):
        rows = pl.ds(pl.multiple_of(i * step, step), step)
        return pltpu.make_async_copy(cal_hbm.at[rows], cal_ref.at[rows], cal_sem.at[i])

    @pl.loop(0, chunks)
    def _(i):
        cal_copy(i).start()

    ul = ulist_ref[...]
    own_row = (ul >> 5).astype(F32)
    local_row = (ul & (UO - 1)).astype(F32)
    down = iota((units, units), 0)
    across = iota((units, units), 1)
    own_col = jnp.sum(jnp.where(down == across, own_row, 0.0), 1, keepdims=True)
    earlier = (own_col == own_row) & (down < across)
    rank = jnp.sum(jnp.where(earlier, 1.0, 0.0), 0, keepdims=True)
    dest = rank * n + own_row
    placed = dest == down.astype(F32)
    entry = jnp.sum(jnp.where(placed, across.astype(F32), 0.0), 1, keepdims=True)
    entry = entry.astype(jnp.int32)
    local = jnp.sum(jnp.where(placed, local_row, 0.0), 1, keepdims=True)
    lane_n = iota((n, LANES), 1)
    names = jnp.zeros((n, LANES), F32)
    for r in range(named):
        names = names + jnp.where(lane_n == r, local[r * n : (r + 1) * n], 0.0)
    send_a[:, 7, :] = names

    for l in range(sources // LANES):
        pmat_ref[l * 8 : l * 8 + 8, :] = jnp.zeros((8, LANES), F32)
        pmat_ref[l * 8 : l * 8 + ASTRO, :] = params_ref[:, l * LANES : (l + 1) * LANES]

    pl.semaphore_wait(barrier, n - 1)
    rim_copy = pltpu.make_async_remote_copy(
        src_ref=coef_ref.at[:, pl.ds(0, LANES)],
        dst_ref=rim_ref,
        send_sem=rim_sems.at[0],
        recv_sem=rim_sems.at[1],
        device_id=(lax.rem(tm + n_time - 1, n_time), sc),
        device_id_type=MESH,
    )
    rim_copy.start()
    rim_copy.wait()
    rim = jnp.where(tm == n_time - 1, 0.0, rim_ref[...])
    ext = jnp.concatenate([coef_ref[...], rim], 1)
    highs = knots // LANES
    for j in range(ORDER):
        for l in range(highs):
            row = (j * highs + l) * QUAT
            amat_ref[row : row + QUAT, :] = ext[:, l * LANES + j : (l + 1) * LANES + j]
    amat = jnp.concatenate(halves(amat_ref[...]), 1)

    block = highs * QUAT
    slot_row = iota((1, CAP), 1)
    lane_col = iota((LANES, step), 0)
    high_col = iota((8, step), 0) // QUAT

    @pl.loop(0, chunks)
    def _(i):
        cols = pl.ds(pl.multiple_of(i * step, step), step)
        mask = jnp.concatenate(
            [(slot_row < cnt_ref[i * GROUP + k]).astype(jnp.int32) for k in range(GROUP)], 1
        )
        mask = mask > 0
        knot = knot_ref[:, cols]
        hot = jnp.where(lane_col == (knot & (LANES - 1)), 1.0, 0.0).astype(BF16)
        got = matmul(amat, jnp.concatenate([hot, hot], 0))
        w = w_ref[:, cols]
        mixed = w[0:1] * got[0:block]
        for j in range(1, ORDER):
            mixed = mixed + w[j : j + 1] * got[j * block : (j + 1) * block]
        high = (knot >> 7) - high_col
        picked = jnp.zeros((8, step), F32)
        for p in range(block // 8):
            picked = picked + jnp.where(high == 2 * p, mixed[p * 8 : p * 8 + 8], 0.0)
        ap = ap_ref[:, cols]
        att = jnp.sum(picked * jnp.concatenate([ap, ap], 0), 0, keepdims=True)
        res = jnp.where(mask, obs_ref[:, cols] - att, 0.0)
        res_ref[:, cols] = res
        live_ref[:, cols] = jnp.where(mask, uslot_ref[:, cols], -1)
        part = jnp.where(mask, sp_ref[:, cols], 0.0)
        ids = ids_ref[:, cols]
        for k in range(GROUP):
            here = slice(k * CAP, (k + 1) * CAP)
            o = i * GROUP + k
            send_a[o, 0:ASTRO, :] = part[:, here]
            send_a[o, 5:6, :] = res[:, here]
            send_a[o, 6:7, :] = (ids[:, here] - o * sources).astype(F32)

    def send(src, dst, sems):
        @pl.loop(1, n)
        def _(s):
            other, where = peer(s)
            pltpu.make_async_remote_copy(
                src_ref=src.at[other],
                dst_ref=dst.at[me],
                send_sem=sems.at[0],
                recv_sem=sems.at[1],
                device_id=where,
                device_id_type=MESH,
            ).start()

        dst[me] = src[me]

    def wait_all(buf, sem):
        most = buf.at[pl.ds(0, n - 1)]
        pltpu.make_async_copy(most, most, sem).wait()

    send(send_a, recv_a, a_sems)

    acc_rhs[...] = jnp.zeros_like(acc_rhs)
    acc_diag[...] = jnp.zeros_like(acc_diag)

    @pl.loop(0, chunks)
    def _(i):
        cols = pl.ds(pl.multiple_of(i * step, step), step)
        hit = live_ref[:, cols] == entry
        weighted = jnp.concatenate(halves(jnp.where(hit, res_ref[:, cols], 0.0)), 0)
        hot = jnp.where(hit, 1.0, 0.0).astype(BF16)
        cal_copy(i).wait()
        cal = cal_ref[cols, :]
        cal_high, cal_low = halves(cal)
        sq_high, sq_low = halves(cal * cal)
        both = matmul(weighted, cal_high)
        acc_rhs[...] += both[:units] + both[units:] + matmul(weighted[:units], cal_low)
        acc_diag[...] += matmul(hot, sq_high) + matmul(hot, sq_low)

    per = width // LANES
    for r in range(named):
        for c in range(per):
            here = slice(c * LANES, (c + 1) * LANES)
            send_b[:, r * 2 * per + c, :] = acc_rhs[r * n : (r + 1) * n, here]
            send_b[:, r * 2 * per + per + c, :] = acc_diag[r * n : (r + 1) * n, here]

    send(send_b, recv_b, b_sems)

    wait_all(recv_a, a_sems.at[1])
    lows = sources // LANES
    pmat = jnp.concatenate(halves(pmat_ref[...]), 1)
    acc_src[...] = jnp.zeros_like(acc_src)
    row8 = iota((8, step), 0)

    @pl.loop(0, chunks)
    def _(i):
        got = jnp.concatenate([recv_a[i * GROUP + k] for k in range(GROUP)], 1)
        ids = got[6:7].astype(jnp.int32)
        hot = jnp.where(lane_col == (ids & (LANES - 1)), 1.0, 0.0).astype(BF16)
        low = ids >> 7
        all_par = matmul(pmat, jnp.concatenate([hot, hot], 0))
        par = jnp.zeros((8, step), F32)
        for l in range(lows):
            par = par + jnp.where(low == l, all_par[l * 8 : l * 8 + 8], 0.0)
        res2 = got[5:6] - jnp.sum(got * par, 0, keepdims=True)
        right = jnp.where(row8 < ASTRO, got, jnp.where(row8 == ASTRO, res2, 0.0))
        prods = jnp.concatenate([got[p : p + 1] * right for p in range(ASTRO)], 0)
        split = jnp.concatenate(halves(prods), 0)
        rows = jnp.concatenate(
            [split * jnp.where(low == l, 1.0, 0.0).astype(BF16) for l in range(lows)], 0
        )
        acc_src[...] += lax.dot_general(
            rows, hot, (((1,), (1,)), ((), ())), preferred_element_type=F32
        )

    size = 8 * ASTRO
    for l in range(lows):
        here = slice(l * LANES, (l + 1) * LANES)
        base = 2 * l * size
        total = acc_src[base : base + size, :] + acc_src[base + size : base + 2 * size, :]
        for p in range(ASTRO):
            gram_ref[p * ASTRO : (p + 1) * ASTRO, here] = total[p * 8 : p * 8 + ASTRO]
            rhs_ref[p : p + 1, here] = total[p * 8 + ASTRO : p * 8 + ASTRO + 1]

    tags = recv_a[:, 7, :]
    same = iota((n, n), 0) == iota((n, n), 1)
    unit_col = iota((UO, n), 0).astype(F32)
    places = []
    for r in range(named):
        tag = jnp.sum(jnp.where(lane_n == r, tags, 0.0), 1, keepdims=True)
        tag_row = jnp.sum(jnp.where(same, tag, 0.0), 0, keepdims=True)
        places.append(jnp.where(tag_row == unit_col, 1.0, 0.0))
    place = jnp.concatenate(places, 1).astype(BF16)

    wait_all(recv_b, b_sems.at[1])
    for c in range(2 * per):
        terms = jnp.concatenate([recv_b[:, r * 2 * per + c, :] for r in range(named)], 0)
        high, rest = terms.astype(BF16), terms
        rest = rest - high.astype(F32)
        middle, last = halves(rest)
        total = matmul(place, high) + (matmul(place, middle) + matmul(place, last))
        here = slice((c % per) * LANES, (c % per + 1) * LANES)
        tiles_ref[:, c // per, here] = total

    wait_all(send_a, a_sems.at[0])
    wait_all(send_b, b_sems.at[0])


def on_device(
    n_time,
    n_src,
    observed,
    att_coef,
    att_partial,
    spline_w,
    knot_idx,
    src_partial,
    src_ids,
    src_params,
    owner_counts,
    cal_partial,
    unit_slot,
    unit_list,
):
    n = n_time * n_src
    transits = observed.shape[0]
    sources = src_params.shape[1]
    knots = att_coef.shape[1]
    units = unit_list.shape[0]
    width = cal_partial.shape[1]
    vmem = pl.BlockSpec(memory_space=pltpu.VMEM)
    return pl.pallas_call(
        functools.partial(kernel, n_time, n_src),
        out_shape=(
            jax.ShapeDtypeStruct((ASTRO * ASTRO, sources), F32),
            jax.ShapeDtypeStruct((ASTRO, sources), F32),
            jax.ShapeDtypeStruct((UO, 2, width), F32),
        ),
        in_specs=[pl.BlockSpec(memory_space=pltpu.SMEM)]
        + [vmem] * 10
        + [pl.BlockSpec(memory_space=pl.ANY)],
        out_specs=(vmem, vmem, vmem),
        scratch_shapes=[
            pltpu.VMEM((transits, width), F32),
            pltpu.VMEM((QUAT, LANES), F32),
            pltpu.VMEM((ORDER * QUAT * knots // LANES, LANES), F32),
            pltpu.VMEM((8 * sources // LANES, LANES), F32),
            pltpu.VMEM((1, transits), F32),
            pltpu.VMEM((1, transits), jnp.int32),
            pltpu.VMEM((units, width), F32),
            pltpu.VMEM((units, width), F32),
            pltpu.VMEM((2 * 8 * ASTRO * sources // LANES, LANES), F32),
            pltpu.VMEM((n, 8, LANES), F32),
            pltpu.VMEM((n, 8, LANES), F32),
            pltpu.VMEM((n, 8, LANES), F32),
            pltpu.VMEM((n, 8, LANES), F32),
            pltpu.SemaphoreType.DMA((transits // (GROUP * CAP),)),
            pltpu.SemaphoreType.DMA((2,)),
            pltpu.SemaphoreType.DMA((2,)),
            pltpu.SemaphoreType.DMA((2,)),
        ],
        compiler_params=pltpu.CompilerParams(
            collective_id=0, has_side_effects=True, vmem_limit_bytes=48 * 1024 * 1024
        ),
    )(
        owner_counts,
        observed.reshape(1, transits),
        att_coef,
        att_partial,
        spline_w,
        knot_idx.reshape(1, transits),
        src_partial,
        src_ids.reshape(1, transits),
        src_params,
        unit_slot.reshape(1, transits),
        unit_list.reshape(1, units),
        cal_partial,
    )


def solution(mesh):
    return jax.shard_map(
        functools.partial(on_device, mesh.shape["tm"], mesh.shape["src"]),
        mesh=mesh,
        in_specs=(
            P(("tm", "src")),
            P(None, "tm"),
            P(None, ("tm", "src")),
            P(None, ("tm", "src")),
            P(("tm", "src")),
            P(None, ("tm", "src")),
            P(("tm", "src")),
            P(None, ("tm", "src")),
            P(("tm", "src")),
            P(("tm", "src"), None),
            P(("tm", "src")),
            P(("tm", "src")),
        ),
        out_specs=(P(None, ("tm", "src")), P(None, ("tm", "src")), P(("tm", "src"), None, None)),
        check_vma=False,
    )
```

```python
import functools

import jax
import jax.numpy as jnp
from jax import lax
from jax.experimental import pallas as pl
from jax.experimental.pallas import tpu as pltpu
from jax.sharding import PartitionSpec as P

ORDER = 4
QUAT = 4
ASTRO = 5
CAP = 128
UO = 32
LANES = 128
SIGNALS = 4
SENDS = 4
UNROLL = 1
GROUP = 16
F32 = jnp.float32
BF16 = jnp.bfloat16
MESH = pl.DeviceIdType.MESH


def halves(x):
    high = x.astype(BF16)
    return high, (x - high.astype(F32)).astype(BF16)


def matmul(a, b):
    return jnp.dot(a, b, preferred_element_type=F32)


def iota(shape, dim):
    return lax.broadcasted_iota(jnp.int32, shape, dim)


def kernel(
    n_time,
    n_src,
    ulist_hbm,
    cnt_hbm,
    uslot_hbm,
    coef_hbm,
    params_hbm,
    knot_hbm,
    ap_hbm,
    w_hbm,
    obs_hbm,
    sp_hbm,
    ids_hbm,
    cal_hbm,
    gram_hbm,
    rhs_hbm,
    tiles_hbm,
    gram_ref,
    rhs_ref,
    tiles_ref,
    ulist_ref,
    cnt_ref,
    uslot_ref,
    coef_ref,
    params_ref,
    knot_ref,
    ap_ref,
    w_ref,
    obs_ref,
    sp_ref,
    ids_ref,
    cal_ref,
    rim_ref,
    amat_ref,
    pmat_ref,
    res_ref,
    live_ref,
    acc_rhs,
    acc_diag,
    acc_src,
    send_a,
    recv_a,
    send_b,
    recv_b,
    in_sems,
    out_sems,
    cal_sem,
    rim_sems,
    a_sems,
    b_sems,
):
    n = n_time * n_src
    tm = lax.axis_index("tm")
    sc = lax.axis_index("src")
    me = tm * n_src + sc
    transits = obs_ref.shape[1]
    sources = params_ref.shape[1]
    knots = coef_ref.shape[1]
    units = ulist_ref.shape[1]
    width = cal_hbm.shape[1]
    named = units // n
    step = GROUP * CAP
    chunks = transits // step

    def place_of(other):
        if n_src & (n_src - 1) == 0:
            return other >> (n_src.bit_length() - 1), other & (n_src - 1)
        return lax.div(other, n_src), lax.rem(other, n_src)

    def peer(s):
        other = (me + s) & (n - 1) if n & (n - 1) == 0 else lax.rem(me + s, n)
        return other, place_of(other)

    barrier = pltpu.get_barrier_semaphore()

    @pl.loop(1, n, unroll=SIGNALS)
    def _(s):
        pl.semaphore_signal(barrier, inc=1, device_id=peer(s)[1], device_id_type=MESH)

    pairs = (
        (ulist_hbm, ulist_ref),
        (cnt_hbm, cnt_ref),
        (uslot_hbm, uslot_ref),
        (coef_hbm, coef_ref),
        (params_hbm, params_ref),
        (knot_hbm, knot_ref),
        (ap_hbm, ap_ref),
        (w_hbm, w_ref),
        (obs_hbm, obs_ref),
        (sp_hbm, sp_ref),
        (ids_hbm, ids_ref),
    )
    ins = [pltpu.make_async_copy(a, b, in_sems.at[k]) for k, (a, b) in enumerate(pairs)]

    def cal_copy(i):
        rows = pl.ds(pl.multiple_of(i * step, step), step)
        return pltpu.make_async_copy(cal_hbm.at[rows], cal_ref.at[rows], cal_sem.at[i])

    for copy in ins[:3]:
        copy.start()
    cal_copy(0).start()
    for copy in ins[3:]:
        copy.start()

    @pl.loop(1, chunks)
    def _(i):
        cal_copy(i).start()

    ins[0].wait()

    ul = ulist_ref[...]
    own_row = (ul >> 5).astype(F32)
    local_row = (ul & (UO - 1)).astype(F32)
    down = iota((units, units), 0)
    across = iota((units, units), 1)
    own_col = jnp.sum(jnp.where(down == across, own_row, 0.0), 1, keepdims=True)
    earlier = (own_col == own_row) & (down < across)
    rank = jnp.sum(jnp.where(earlier, 1.0, 0.0), 0, keepdims=True)
    dest = rank * n + own_row
    placed = dest == down.astype(F32)
    entry = jnp.sum(jnp.where(placed, across.astype(F32), 0.0), 1, keepdims=True)
    entry = entry.astype(jnp.int32)
    local = jnp.sum(jnp.where(placed, local_row, 0.0), 1, keepdims=True)
    lane_n = iota((n, LANES), 1)
    names = jnp.zeros((n, LANES), F32)
    for r in range(named):
        names = names + jnp.where(lane_n == r, local[r * n : (r + 1) * n], 0.0)
    send_a[:, 7, :] = names

    ins[3].wait()
    pl.semaphore_wait(barrier, n - 1)
    rim_copy = pltpu.make_async_remote_copy(
        src_ref=coef_ref.at[:, pl.ds(0, LANES)],
        dst_ref=rim_ref,
        send_sem=rim_sems.at[0],
        recv_sem=rim_sems.at[1],
        device_id=(lax.rem(tm + n_time - 1, n_time), sc),
        device_id_type=MESH,
    )
    rim_copy.start()

    acc_diag[...] = jnp.zeros_like(acc_diag)
    slot_row = iota((1, CAP), 1)
    ins[1].wait()
    ins[2].wait()

    def diag(i):
        cols = pl.ds(pl.multiple_of(i * step, step), step)
        mask = jnp.concatenate(
            [(slot_row < cnt_ref[i * GROUP + k]).astype(jnp.int32) for k in range(GROUP)], 1
        )
        live = jnp.where(mask > 0, uslot_ref[:, cols], -1)
        live_ref[:, cols] = live
        hot = jnp.where(live == entry, 1.0, 0.0).astype(BF16)
        cal_copy(i).wait()
        cal = cal_ref[cols, :]
        sq_high, sq_low = halves(cal * cal)
        acc_diag[...] += matmul(hot, sq_high) + matmul(hot, sq_low)

    pl.loop(0, chunks, unroll=UNROLL)(diag)

    for copy in ins[4:]:
        copy.wait()
    for l in range(sources // LANES):
        pmat_ref[l * 8 : l * 8 + 8, :] = jnp.zeros((8, LANES), F32)
        pmat_ref[l * 8 : l * 8 + ASTRO, :] = params_ref[:, l * LANES : (l + 1) * LANES]

    rim_copy.wait()
    rim = jnp.where(tm == n_time - 1, 0.0, rim_ref[...])
    ext = jnp.concatenate([coef_ref[...], rim], 1)
    highs = knots // LANES
    for j in range(ORDER):
        for l in range(highs):
            row = (j * highs + l) * QUAT
            amat_ref[row : row + QUAT, :] = ext[:, l * LANES + j : (l + 1) * LANES + j]
    amat = jnp.concatenate(halves(amat_ref[...]), 1)

    block = highs * QUAT
    lane_col = iota((LANES, step), 0)
    high_col = iota((8, step), 0) // QUAT

    def attitude(i):
        cols = pl.ds(pl.multiple_of(i * step, step), step)
        mask = live_ref[:, cols] >= 0
        knot = knot_ref[:, cols]
        hot = jnp.where(lane_col == (knot & (LANES - 1)), 1.0, 0.0).astype(BF16)
        got = matmul(amat, jnp.concatenate([hot, hot], 0))
        w = w_ref[:, cols]
        mixed = w[0:1] * got[0:block]
        for j in range(1, ORDER):
            mixed = mixed + w[j : j + 1] * got[j * block : (j + 1) * block]
        high = (knot >> 7) - high_col
        picked = jnp.zeros((8, step), F32)
        for p in range(block // 8):
            picked = picked + jnp.where(high == 2 * p, mixed[p * 8 : p * 8 + 8], 0.0)
        ap = ap_ref[:, cols]
        att = jnp.sum(picked * jnp.concatenate([ap, ap], 0), 0, keepdims=True)
        res = jnp.where(mask, obs_ref[:, cols] - att, 0.0)
        res_ref[:, cols] = res
        part = jnp.where(mask, sp_ref[:, cols], 0.0)
        ids = ids_ref[:, cols]
        for k in range(GROUP):
            here = slice(k * CAP, (k + 1) * CAP)
            o = i * GROUP + k
            send_a[o, 0:ASTRO, :] = part[:, here]
            send_a[o, 5:6, :] = res[:, here]
            send_a[o, 6:7, :] = (ids[:, here] - o * sources).astype(F32)

    pl.loop(0, chunks, unroll=UNROLL)(attitude)

    def send(src, dst, sems):
        @pl.loop(1, n, unroll=SENDS)
        def _(s):
            other, where = peer(s)
            pltpu.make_async_remote_copy(
                src_ref=src.at[other],
                dst_ref=dst.at[me],
                send_sem=sems.at[0],
                recv_sem=sems.at[1],
                device_id=where,
                device_id_type=MESH,
            ).start()

        dst[me] = src[me]

    def wait_all(buf, sem):
        most = buf.at[pl.ds(0, n - 1)]
        pltpu.make_async_copy(most, most, sem).wait()

    send(send_a, recv_a, a_sems)

    acc_rhs[...] = jnp.zeros_like(acc_rhs)

    def right_sides(i):
        cols = pl.ds(pl.multiple_of(i * step, step), step)
        hit = live_ref[:, cols] == entry
        weighted = jnp.concatenate(halves(jnp.where(hit, res_ref[:, cols], 0.0)), 0)
        cal_high, cal_low = halves(cal_ref[cols, :])
        both = matmul(weighted, cal_high)
        acc_rhs[...] += both[:units] + both[units:] + matmul(weighted[:units], cal_low)

    pl.loop(0, chunks, unroll=UNROLL)(right_sides)

    per = width // LANES
    for r in range(named):
        for c in range(per):
            here = slice(c * LANES, (c + 1) * LANES)
            send_b[:, r * 2 * per + c, :] = acc_rhs[r * n : (r + 1) * n, here]
            send_b[:, r * 2 * per + per + c, :] = acc_diag[r * n : (r + 1) * n, here]

    send(send_b, recv_b, b_sems)

    wait_all(recv_a, a_sems.at[1])
    lows = sources // LANES
    pmat = jnp.concatenate(halves(pmat_ref[...]), 1)
    acc_src[...] = jnp.zeros_like(acc_src)
    row8 = iota((8, step), 0)

    def normals(i):
        got = jnp.concatenate([recv_a[i * GROUP + k] for k in range(GROUP)], 1)
        ids = got[6:7].astype(jnp.int32)
        hot = jnp.where(lane_col == (ids & (LANES - 1)), 1.0, 0.0).astype(BF16)
        low = ids >> 7
        all_par = matmul(pmat, jnp.concatenate([hot, hot], 0))
        par = jnp.zeros((8, step), F32)
        for l in range(lows):
            par = par + jnp.where(low == l, all_par[l * 8 : l * 8 + 8], 0.0)
        res2 = got[5:6] - jnp.sum(got * par, 0, keepdims=True)
        right = jnp.where(row8 < ASTRO, got, jnp.where(row8 == ASTRO, res2, 0.0))
        prods = jnp.concatenate([got[p : p + 1] * right for p in range(ASTRO)], 0)
        split = jnp.concatenate(halves(prods), 0)
        rows = jnp.concatenate(
            [split * jnp.where(low == l, 1.0, 0.0).astype(BF16) for l in range(lows)], 0
        )
        acc_src[...] += lax.dot_general(
            rows, hot, (((1,), (1,)), ((), ())), preferred_element_type=F32
        )

    pl.loop(0, chunks, unroll=UNROLL)(normals)

    size = 8 * ASTRO
    for l in range(lows):
        here = slice(l * LANES, (l + 1) * LANES)
        base = 2 * l * size
        total = acc_src[base : base + size, :] + acc_src[base + size : base + 2 * size, :]
        for p in range(ASTRO):
            gram_ref[p * ASTRO : (p + 1) * ASTRO, here] = total[p * 8 : p * 8 + ASTRO]
            rhs_ref[p : p + 1, here] = total[p * 8 + ASTRO : p * 8 + ASTRO + 1]

    outs = (
        pltpu.make_async_copy(gram_ref, gram_hbm, out_sems.at[0]),
        pltpu.make_async_copy(rhs_ref, rhs_hbm, out_sems.at[1]),
        pltpu.make_async_copy(tiles_ref, tiles_hbm, out_sems.at[2]),
    )
    outs[0].start()
    outs[1].start()

    tags = recv_a[:, 7, :]
    same = iota((n, n), 0) == iota((n, n), 1)
    unit_col = iota((UO, n), 0).astype(F32)
    places = []
    for r in range(named):
        tag = jnp.sum(jnp.where(lane_n == r, tags, 0.0), 1, keepdims=True)
        tag_row = jnp.sum(jnp.where(same, tag, 0.0), 0, keepdims=True)
        places.append(jnp.where(tag_row == unit_col, 1.0, 0.0))
    place = jnp.concatenate(places, 1).astype(BF16)

    wait_all(recv_b, b_sems.at[1])
    for c in range(2 * per):
        terms = jnp.concatenate([recv_b[:, r * 2 * per + c, :] for r in range(named)], 0)
        high, rest = terms.astype(BF16), terms
        rest = rest - high.astype(F32)
        middle, last = halves(rest)
        total = matmul(place, high) + (matmul(place, middle) + matmul(place, last))
        here = slice((c % per) * LANES, (c % per + 1) * LANES)
        tiles_ref[:, c // per, here] = total

    outs[2].start()
    wait_all(send_a, a_sems.at[0])
    wait_all(send_b, b_sems.at[0])
    for copy in outs:
        copy.wait()


def hand_over(*refs):
    ins, outs, held, sems = refs[:3], refs[3:6], refs[6:9], refs[9]
    first = [pltpu.make_async_copy(ins[k], held[k], sems.at[k]) for k in range(3)]
    second = [pltpu.make_async_copy(held[k], outs[k], sems.at[k]) for k in range(3)]
    for copy in first:
        copy.start()
    for k in range(3):
        first[k].wait()
        second[k].start()
    for copy in second:
        copy.wait()


def on_device(
    n_time,
    n_src,
    observed,
    att_coef,
    att_partial,
    spline_w,
    knot_idx,
    src_partial,
    src_ids,
    src_params,
    owner_counts,
    cal_partial,
    unit_slot,
    unit_list,
):
    n = n_time * n_src
    transits = observed.shape[0]
    sources = src_params.shape[1]
    knots = att_coef.shape[1]
    units = unit_list.shape[0]
    width = cal_partial.shape[1]
    hbm = pl.BlockSpec(memory_space=pltpu.HBM)
    shapes = ((ASTRO * ASTRO, sources), (ASTRO, sources), (UO, 2, width))
    out_shape = tuple(jax.ShapeDtypeStruct(shape, F32) for shape in shapes)
    results = pl.pallas_call(
        functools.partial(kernel, n_time, n_src),
        out_shape=out_shape,
        in_specs=[hbm] * 12,
        out_specs=(hbm, hbm, hbm),
        scratch_shapes=[pltpu.VMEM(shape, F32) for shape in shapes]
        + [
            pltpu.VMEM((1, units), jnp.int32),
            pltpu.SMEM((n,), jnp.int32),
            pltpu.VMEM((1, transits), jnp.int32),
            pltpu.VMEM((QUAT, knots), F32),
            pltpu.VMEM((ASTRO, sources), F32),
            pltpu.VMEM((1, transits), jnp.int32),
            pltpu.VMEM((QUAT, transits), F32),
            pltpu.VMEM((ORDER, transits), F32),
            pltpu.VMEM((1, transits), F32),
            pltpu.VMEM((ASTRO, transits), F32),
            pltpu.VMEM((1, transits), jnp.int32),
            pltpu.VMEM((transits, width), F32),
            pltpu.VMEM((QUAT, LANES), F32),
            pltpu.VMEM((ORDER * QUAT * knots // LANES, LANES), F32),
            pltpu.VMEM((8 * sources // LANES, LANES), F32),
            pltpu.VMEM((1, transits), F32),
            pltpu.VMEM((1, transits), jnp.int32),
            pltpu.VMEM((units, width), F32),
            pltpu.VMEM((units, width), F32),
            pltpu.VMEM((2 * 8 * ASTRO * sources // LANES, LANES), F32),
            pltpu.VMEM((n, 8, LANES), F32),
            pltpu.VMEM((n, 8, LANES), F32),
            pltpu.VMEM((n, 8, LANES), F32),
            pltpu.VMEM((n, 8, LANES), F32),
            pltpu.SemaphoreType.DMA((11,)),
            pltpu.SemaphoreType.DMA((3,)),
            pltpu.SemaphoreType.DMA((transits // (GROUP * CAP),)),
            pltpu.SemaphoreType.DMA((2,)),
            pltpu.SemaphoreType.DMA((2,)),
            pltpu.SemaphoreType.DMA((2,)),
        ],
        compiler_params=pltpu.CompilerParams(
            collective_id=0, has_side_effects=True, vmem_limit_bytes=64 * 1024 * 1024
        ),
    )(
        unit_list.reshape(1, units),
        owner_counts,
        unit_slot.reshape(1, transits),
        att_coef,
        src_params,
        knot_idx.reshape(1, transits),
        att_partial,
        spline_w,
        observed.reshape(1, transits),
        src_partial,
        src_ids.reshape(1, transits),
        cal_partial,
    )
    return pl.pallas_call(
        hand_over,
        out_shape=out_shape,
        in_specs=[hbm] * 3,
        out_specs=(hbm, hbm, hbm),
        scratch_shapes=[pltpu.VMEM(shape, F32) for shape in shapes]
        + [pltpu.SemaphoreType.DMA((3,))],
        compiler_params=pltpu.CompilerParams(vmem_limit_bytes=64 * 1024 * 1024),
    )(*results)


def solution(mesh):
    return jax.shard_map(
        functools.partial(on_device, mesh.shape["tm"], mesh.shape["src"]),
        mesh=mesh,
        in_specs=(
            P(("tm", "src")),
            P(None, "tm"),
            P(None, ("tm", "src")),
            P(None, ("tm", "src")),
            P(("tm", "src")),
            P(None, ("tm", "src")),
            P(("tm", "src")),
            P(None, ("tm", "src")),
            P(("tm", "src")),
            P(("tm", "src"), None),
            P(("tm", "src")),
            P(("tm", "src")),
        ),
        out_specs=(P(None, ("tm", "src")), P(None, ("tm", "src")), P(("tm", "src"), None, None)),
        check_vma=False,
    )
```

```python
import functools

import jax
import jax.numpy as jnp
from jax import lax
from jax.experimental import pallas as pl
from jax.experimental.pallas import tpu as pltpu
from jax.sharding import PartitionSpec as P

ORDER = 4
QUAT = 4
ASTRO = 5
CAP = 128
UO = 32
LANES = 128
SIGNALS = 4
SENDS = 4
UNROLL = 1
GROUP = 32
F32 = jnp.float32
BF16 = jnp.bfloat16
MESH = pl.DeviceIdType.MESH


def halves(x):
    high = x.astype(BF16)
    return high, (x - high.astype(F32)).astype(BF16)


def matmul(a, b):
    return jnp.dot(a, b, preferred_element_type=F32)


def iota(shape, dim):
    return lax.broadcasted_iota(jnp.int32, shape, dim)


def kernel(
    n_time,
    n_src,
    ulist_hbm,
    cnt_hbm,
    uslot_hbm,
    coef_hbm,
    params_hbm,
    knot_hbm,
    ap_hbm,
    w_hbm,
    obs_hbm,
    sp_hbm,
    ids_hbm,
    cal_hbm,
    gram_hbm,
    rhs_hbm,
    recv_b,
    place_hbm,
    gram_ref,
    rhs_ref,
    place_ref,
    ulist_ref,
    cnt_ref,
    uslot_ref,
    coef_ref,
    params_ref,
    knot_ref,
    ap_ref,
    w_ref,
    obs_ref,
    sp_ref,
    ids_ref,
    cal_ref,
    rim_ref,
    amat_ref,
    pmat_ref,
    res_ref,
    live_ref,
    acc_rhs,
    acc_diag,
    acc_src,
    send_a,
    recv_a,
    send_b,
    in_sems,
    out_sems,
    cal_sem,
    rim_sems,
    a_sems,
    b_sems,
):
    n = n_time * n_src
    tm = lax.axis_index("tm")
    sc = lax.axis_index("src")
    me = tm * n_src + sc
    transits = obs_ref.shape[1]
    sources = params_ref.shape[1]
    knots = coef_ref.shape[1]
    units = ulist_ref.shape[1]
    width = cal_hbm.shape[1]
    named = units // n
    step = GROUP * CAP
    chunks = transits // step

    def place_of(other):
        if n_src & (n_src - 1) == 0:
            return other >> (n_src.bit_length() - 1), other & (n_src - 1)
        return lax.div(other, n_src), lax.rem(other, n_src)

    def peer(s):
        other = (me + s) & (n - 1) if n & (n - 1) == 0 else lax.rem(me + s, n)
        return other, place_of(other)

    barrier = pltpu.get_barrier_semaphore()

    pairs = (
        (ulist_hbm, ulist_ref),
        (cnt_hbm, cnt_ref),
        (uslot_hbm, uslot_ref),
        (coef_hbm, coef_ref),
        (params_hbm, params_ref),
        (knot_hbm, knot_ref),
        (ap_hbm, ap_ref),
        (w_hbm, w_ref),
        (obs_hbm, obs_ref),
        (sp_hbm, sp_ref),
        (ids_hbm, ids_ref),
    )
    ins = [pltpu.make_async_copy(a, b, in_sems.at[k]) for k, (a, b) in enumerate(pairs)]

    def cal_copy(i):
        rows = pl.ds(pl.multiple_of(i * step, step), step)
        return pltpu.make_async_copy(cal_hbm.at[rows], cal_ref.at[rows], cal_sem.at[i])

    for copy in ins[:3]:
        copy.start()
    cal_copy(0).start()
    for copy in ins[3:]:
        copy.start()

    @pl.loop(1, chunks)
    def _(i):
        cal_copy(i).start()

    @pl.loop(1, n, unroll=SIGNALS)
    def _(s):
        pl.semaphore_signal(barrier, inc=1, device_id=peer(s)[1], device_id_type=MESH)

    ins[0].wait()

    ul = ulist_ref[...]
    own_row = (ul >> 5).astype(F32)
    local_row = (ul & (UO - 1)).astype(F32)
    down = iota((units, units), 0)
    across = iota((units, units), 1)
    own_col = jnp.sum(jnp.where(down == across, own_row, 0.0), 1, keepdims=True)
    earlier = (own_col == own_row) & (down < across)
    rank = jnp.sum(jnp.where(earlier, 1.0, 0.0), 0, keepdims=True)
    dest = rank * n + own_row
    placed = dest == down.astype(F32)
    entry = jnp.sum(jnp.where(placed, across.astype(F32), 0.0), 1, keepdims=True)
    entry = entry.astype(jnp.int32)
    local = jnp.sum(jnp.where(placed, local_row, 0.0), 1, keepdims=True)
    lane_n = iota((n, LANES), 1)
    names = jnp.zeros((n, LANES), F32)
    for r in range(named):
        names = names + jnp.where(lane_n == r, local[r * n : (r + 1) * n], 0.0)
    send_a[:, 7, :] = names

    ins[3].wait()
    pl.semaphore_wait(barrier, n - 1)
    rim_copy = pltpu.make_async_remote_copy(
        src_ref=coef_ref.at[:, pl.ds(0, LANES)],
        dst_ref=rim_ref,
        send_sem=rim_sems.at[0],
        recv_sem=rim_sems.at[1],
        device_id=(lax.rem(tm + n_time - 1, n_time), sc),
        device_id_type=MESH,
    )
    rim_copy.start()

    acc_diag[...] = jnp.zeros_like(acc_diag)
    slot_row = iota((1, CAP), 1)
    ins[1].wait()
    ins[2].wait()

    def diag(i):
        cols = pl.ds(pl.multiple_of(i * step, step), step)
        mask = jnp.concatenate(
            [(slot_row < cnt_ref[i * GROUP + k]).astype(jnp.int32) for k in range(GROUP)], 1
        )
        live = jnp.where(mask > 0, uslot_ref[:, cols], -1)
        live_ref[:, cols] = live
        hot = jnp.where(live == entry, 1.0, 0.0).astype(BF16)
        cal_copy(i).wait()
        cal = cal_ref[cols, :]
        sq_high, sq_low = halves(cal * cal)
        acc_diag[...] += matmul(hot, sq_high) + matmul(hot, sq_low)

    pl.loop(0, chunks, unroll=UNROLL)(diag)

    for copy in ins[4:]:
        copy.wait()
    for l in range(sources // LANES):
        pmat_ref[l * 8 : l * 8 + 8, :] = jnp.zeros((8, LANES), F32)
        pmat_ref[l * 8 : l * 8 + ASTRO, :] = params_ref[:, l * LANES : (l + 1) * LANES]

    rim_copy.wait()
    rim = jnp.where(tm == n_time - 1, 0.0, rim_ref[...])
    ext = jnp.concatenate([coef_ref[...], rim], 1)
    highs = knots // LANES
    for j in range(ORDER):
        for l in range(highs):
            row = (j * highs + l) * QUAT
            amat_ref[row : row + QUAT, :] = ext[:, l * LANES + j : (l + 1) * LANES + j]
    amat = jnp.concatenate(halves(amat_ref[...]), 1)

    block = highs * QUAT
    lane_col = iota((LANES, step), 0)
    high_col = iota((8, step), 0) // QUAT

    def attitude(i):
        cols = pl.ds(pl.multiple_of(i * step, step), step)
        mask = live_ref[:, cols] >= 0
        knot = knot_ref[:, cols]
        hot = jnp.where(lane_col == (knot & (LANES - 1)), 1.0, 0.0).astype(BF16)
        got = matmul(amat, jnp.concatenate([hot, hot], 0))
        w = w_ref[:, cols]
        mixed = w[0:1] * got[0:block]
        for j in range(1, ORDER):
            mixed = mixed + w[j : j + 1] * got[j * block : (j + 1) * block]
        high = (knot >> 7) - high_col
        picked = jnp.zeros((8, step), F32)
        for p in range(block // 8):
            picked = picked + jnp.where(high == 2 * p, mixed[p * 8 : p * 8 + 8], 0.0)
        ap = ap_ref[:, cols]
        att = jnp.sum(picked * jnp.concatenate([ap, ap], 0), 0, keepdims=True)
        res = jnp.where(mask, obs_ref[:, cols] - att, 0.0)
        res_ref[:, cols] = res
        part = jnp.where(mask, sp_ref[:, cols], 0.0)
        ids = ids_ref[:, cols]
        for k in range(GROUP):
            here = slice(k * CAP, (k + 1) * CAP)
            o = i * GROUP + k
            send_a[o, 0:ASTRO, :] = part[:, here]
            send_a[o, 5:6, :] = res[:, here]
            send_a[o, 6:7, :] = (ids[:, here] - o * sources).astype(F32)

    pl.loop(0, chunks, unroll=UNROLL)(attitude)

    def send(src, dst, sems, own=True):
        @pl.loop(1, n, unroll=SENDS)
        def _(s):
            other, where = peer(s)
            pltpu.make_async_remote_copy(
                src_ref=src.at[other],
                dst_ref=dst.at[me],
                send_sem=sems.at[0],
                recv_sem=sems.at[1],
                device_id=where,
                device_id_type=MESH,
            ).start()

        if own:
            dst[me] = src[me]

    def wait_all(buf, sem):
        most = buf.at[pl.ds(0, n - 1)]
        pltpu.make_async_copy(most, most, sem).wait()

    send(send_a, recv_a, a_sems)

    acc_rhs[...] = jnp.zeros_like(acc_rhs)

    def right_sides(i):
        cols = pl.ds(pl.multiple_of(i * step, step), step)
        hit = live_ref[:, cols] == entry
        weighted = jnp.concatenate(halves(jnp.where(hit, res_ref[:, cols], 0.0)), 0)
        cal_high, cal_low = halves(cal_ref[cols, :])
        both = matmul(weighted, cal_high)
        acc_rhs[...] += both[:units] + both[units:] + matmul(weighted[:units], cal_low)

    pl.loop(0, chunks, unroll=UNROLL)(right_sides)

    per = width // LANES
    for r in range(named):
        for c in range(per):
            here = slice(c * LANES, (c + 1) * LANES)
            send_b[:, r * 2 * per + c, :] = acc_rhs[r * n : (r + 1) * n, here]
            send_b[:, r * 2 * per + per + c, :] = acc_diag[r * n : (r + 1) * n, here]

    send(send_b, recv_b, b_sems, False)

    wait_all(recv_a, a_sems.at[1])
    lows = sources // LANES
    pmat = jnp.concatenate(halves(pmat_ref[...]), 1)
    acc_src[...] = jnp.zeros_like(acc_src)
    row8 = iota((8, step), 0)

    def normals(i):
        got = jnp.concatenate([recv_a[i * GROUP + k] for k in range(GROUP)], 1)
        ids = got[6:7].astype(jnp.int32)
        hot = jnp.where(lane_col == (ids & (LANES - 1)), 1.0, 0.0).astype(BF16)
        low = ids >> 7
        all_par = matmul(pmat, jnp.concatenate([hot, hot], 0))
        par = jnp.zeros((8, step), F32)
        for l in range(lows):
            par = par + jnp.where(low == l, all_par[l * 8 : l * 8 + 8], 0.0)
        res2 = got[5:6] - jnp.sum(got * par, 0, keepdims=True)
        right = jnp.where(row8 < ASTRO, got, jnp.where(row8 == ASTRO, res2, 0.0))
        prods = jnp.concatenate([got[p : p + 1] * right for p in range(ASTRO)], 0)
        split = jnp.concatenate(halves(prods), 0)
        rows = jnp.concatenate(
            [split * jnp.where(low == l, 1.0, 0.0).astype(BF16) for l in range(lows)], 0
        )
        acc_src[...] += lax.dot_general(
            rows, hot, (((1,), (1,)), ((), ())), preferred_element_type=F32
        )

    pl.loop(0, chunks, unroll=UNROLL)(normals)

    size = 8 * ASTRO
    for l in range(lows):
        here = slice(l * LANES, (l + 1) * LANES)
        base = 2 * l * size
        total = acc_src[base : base + size, :] + acc_src[base + size : base + 2 * size, :]
        for p in range(ASTRO):
            gram_ref[p * ASTRO : (p + 1) * ASTRO, here] = total[p * 8 : p * 8 + ASTRO]
            rhs_ref[p : p + 1, here] = total[p * 8 + ASTRO : p * 8 + ASTRO + 1]

    outs = (
        pltpu.make_async_copy(gram_ref, gram_hbm, out_sems.at[0]),
        pltpu.make_async_copy(rhs_ref, rhs_hbm, out_sems.at[1]),
        pltpu.make_async_copy(place_ref, place_hbm, out_sems.at[2]),
        pltpu.make_async_copy(send_b.at[me], recv_b.at[me], out_sems.at[3]),
    )
    outs[0].start()
    outs[1].start()

    tags = recv_a[:, 7, :]
    same = iota((n, n), 0) == iota((n, n), 1)
    unit_col = iota((UO, n), 0).astype(F32)
    places = []
    for r in range(named):
        tag = jnp.sum(jnp.where(lane_n == r, tags, 0.0), 1, keepdims=True)
        tag_row = jnp.sum(jnp.where(same, tag, 0.0), 0, keepdims=True)
        places.append(jnp.where(tag_row == unit_col, 1.0, 0.0))
    place_ref[...] = jnp.concatenate(places, 1)
    outs[2].start()
    outs[3].start()

    wait_all(recv_b, b_sems.at[1])
    wait_all(send_a, a_sems.at[0])
    wait_all(send_b, b_sems.at[0])
    for copy in outs:
        copy.wait()


def place_tiles(*refs):
    ins, outs, held, tiles_ref, sems = refs[:4], refs[4:7], refs[7:11], refs[11], refs[12]
    got, place_ref = held[2:]
    first = [pltpu.make_async_copy(ins[k], held[k], sems.at[k]) for k in range(4)]
    second = [
        pltpu.make_async_copy(held[0], outs[0], sems.at[4]),
        pltpu.make_async_copy(held[1], outs[1], sems.at[5]),
        pltpu.make_async_copy(tiles_ref, outs[2], sems.at[6]),
    ]
    for k in (2, 3, 0, 1):
        first[k].start()
    first[2].wait()
    first[3].wait()
    place = place_ref[...].astype(BF16)
    named = place.shape[1] // got.shape[0]
    per = tiles_ref.shape[2] // LANES
    for c in range(2 * per):
        terms = jnp.concatenate([got[:, r * 2 * per + c, :] for r in range(named)], 0)
        high = terms.astype(BF16)
        middle, last = halves(terms - high.astype(F32))
        total = matmul(place, high) + (matmul(place, middle) + matmul(place, last))
        here = slice((c % per) * LANES, (c % per + 1) * LANES)
        tiles_ref[:, c // per, here] = total
    second[2].start()
    for k in range(2):
        first[k].wait()
        second[k].start()
    for copy in second:
        copy.wait()


def on_device(
    n_time,
    n_src,
    observed,
    att_coef,
    att_partial,
    spline_w,
    knot_idx,
    src_partial,
    src_ids,
    src_params,
    owner_counts,
    cal_partial,
    unit_slot,
    unit_list,
):
    n = n_time * n_src
    transits = observed.shape[0]
    sources = src_params.shape[1]
    knots = att_coef.shape[1]
    units = unit_list.shape[0]
    width = cal_partial.shape[1]
    hbm = pl.BlockSpec(memory_space=pltpu.HBM)
    shapes = ((ASTRO * ASTRO, sources), (ASTRO, sources), (n, 8, LANES), (UO, units))
    whole = shapes[:2] + ((UO, 2, width),)

    def struct(sizes):
        return tuple(jax.ShapeDtypeStruct(shape, F32) for shape in sizes)

    results = pl.pallas_call(
        functools.partial(kernel, n_time, n_src),
        out_shape=struct(shapes),
        in_specs=[hbm] * 12,
        out_specs=(hbm, hbm, hbm, hbm),
        scratch_shapes=[pltpu.VMEM(shape, F32) for shape in shapes[:2] + shapes[3:]]
        + [
            pltpu.VMEM((1, units), jnp.int32),
            pltpu.SMEM((n,), jnp.int32),
            pltpu.VMEM((1, transits), jnp.int32),
            pltpu.VMEM((QUAT, knots), F32),
            pltpu.VMEM((ASTRO, sources), F32),
            pltpu.VMEM((1, transits), jnp.int32),
            pltpu.VMEM((QUAT, transits), F32),
            pltpu.VMEM((ORDER, transits), F32),
            pltpu.VMEM((1, transits), F32),
            pltpu.VMEM((ASTRO, transits), F32),
            pltpu.VMEM((1, transits), jnp.int32),
            pltpu.VMEM((transits, width), F32),
            pltpu.VMEM((QUAT, LANES), F32),
            pltpu.VMEM((ORDER * QUAT * knots // LANES, LANES), F32),
            pltpu.VMEM((8 * sources // LANES, LANES), F32),
            pltpu.VMEM((1, transits), F32),
            pltpu.VMEM((1, transits), jnp.int32),
            pltpu.VMEM((units, width), F32),
            pltpu.VMEM((units, width), F32),
            pltpu.VMEM((2 * 8 * ASTRO * sources // LANES, LANES), F32),
            pltpu.VMEM((n, 8, LANES), F32),
            pltpu.VMEM((n, 8, LANES), F32),
            pltpu.VMEM((n, 8, LANES), F32),
            pltpu.SemaphoreType.DMA((11,)),
            pltpu.SemaphoreType.DMA((4,)),
            pltpu.SemaphoreType.DMA((transits // (GROUP * CAP),)),
            pltpu.SemaphoreType.DMA((2,)),
            pltpu.SemaphoreType.DMA((2,)),
            pltpu.SemaphoreType.DMA((2,)),
        ],
        compiler_params=pltpu.CompilerParams(
            collective_id=0, has_side_effects=True, vmem_limit_bytes=64 * 1024 * 1024
        ),
    )(
        unit_list.reshape(1, units),
        owner_counts,
        unit_slot.reshape(1, transits),
        att_coef,
        src_params,
        knot_idx.reshape(1, transits),
        att_partial,
        spline_w,
        observed.reshape(1, transits),
        src_partial,
        src_ids.reshape(1, transits),
        cal_partial,
    )
    return pl.pallas_call(
        place_tiles,
        out_shape=struct(whole),
        in_specs=[hbm] * 4,
        out_specs=(hbm, hbm, hbm),
        scratch_shapes=[pltpu.VMEM(shape, F32) for shape in shapes + whole[2:]]
        + [pltpu.SemaphoreType.DMA((7,))],
        compiler_params=pltpu.CompilerParams(vmem_limit_bytes=64 * 1024 * 1024),
    )(*results)


def solution(mesh):
    return jax.shard_map(
        functools.partial(on_device, mesh.shape["tm"], mesh.shape["src"]),
        mesh=mesh,
        in_specs=(
            P(("tm", "src")),
            P(None, "tm"),
            P(None, ("tm", "src")),
            P(None, ("tm", "src")),
            P(("tm", "src")),
            P(None, ("tm", "src")),
            P(("tm", "src")),
            P(None, ("tm", "src")),
            P(("tm", "src")),
            P(("tm", "src"), None),
            P(("tm", "src")),
            P(("tm", "src")),
        ),
        out_specs=(P(None, ("tm", "src")), P(None, ("tm", "src")), P(("tm", "src"), None, None)),
        check_vma=False,
    )
```
